256 devices in a mesh: blk: 64 (over y_lo, x, z), rep: 4 (over y_hi, core).
Axes of the slice: x: 4, y: 4 (y_hi: 2, y_lo: 2; y = y_hi * 2 + y_lo), z: 8, core: 2. Of those that a mesh axis runs over, the one named last changes fastest.
Arguments:
- node_features: bfloat16 [512, 65536], P('rep', 'blk'), may hold values from -6 to 6
- weight_first: bfloat16 [512, 512], P('rep'), may hold values from -0.25 to 0.25
- weight_second: bfloat16 [512, 512], P('rep'), may hold values from -0.25 to 0.25
- tiles: bfloat16 [256, 6, 256, 256], P('blk'), may hold values from -0.375 to 0.375
- slot_blocks: int32 [256, 6], P('blk'), may hold values from 0 to 255, as said below
- degrees: int32 [256], P('blk'), may hold values from 1 to 6, as said below
- block_position: int32 [256], replicated, may hold values from 0 to 255, as said below
- cotangent: bfloat16 [512, 65536], P('rep', 'blk'), may hold values from -6 to 6
Outputs:
- layer_output: bfloat16 [512, 65536], P('rep', 'blk')
- grad_first: float32 [512, 512], P('rep')
- grad_second: float32 [512, 512], P('rep')
The draws below stay inside these ranges and needn't reach their ends.
Inputs may be any that keep to these rules, and one draw needn't show every extreme that they name: block_position[slot_blocks[b, 0]] = b. For every slot, block_position[slot_blocks[b, t]] // 4 differs from b // 4 by at most 2 modulo 256 // 4. Slots t >= degrees[b] are unused; the value 6 occurs. `block_position`: A permutation of 0 to 255.
All inputs are finite; a program needn't handle non-finite values.
Results may differ from the reference program's by a relative error of at most 0.025.
Values may be sent and summed in bfloat16 or wider, within the bound.
No kernel may reach another device: no remote copies, remote signals or barrier semaphores. Data moves between devices by JAX's collectives and lax.ppermute only.
A program may use at most 64 MiB of HBM per device.

```python
import jax
import jax.numpy as jnp
from jax import lax

WIDTH = 512
BLOCK = 256
SLOTS = 6
BLOCKS_DEV = 4
REACH = 2
BLOCKS = 256
NODES = 65536
N_REP = 4


def shared_positions(key):
    return jax.random.permutation(key, BLOCKS).astype(jnp.int32)


def draw_block_position(key, part):
    positions = shared_positions(key)
    return positions


def draw_slot_blocks(key, part):
    positions = shared_positions(key)
    key = jax.random.fold_in(key, 5)
    initial_of = jnp.argsort(positions, stable=True).astype(jnp.int32)
    shift_key, inner_key = jax.random.split(key)
    devices = BLOCKS // BLOCKS_DEV
    offsets = jax.random.randint(shift_key, (BLOCKS, SLOTS), -REACH, REACH + 1)
    inner = jax.random.randint(inner_key, (BLOCKS, SLOTS), 0, BLOCKS_DEV)
    rows = jnp.arange(BLOCKS, dtype=jnp.int32)
    owners = rows // BLOCKS_DEV
    targets = (owners[:, None] + offsets) % devices * BLOCKS_DEV + inner
    targets = targets.at[:, 0].set(rows)
    return initial_of[targets].astype(jnp.int32)


def draw_degrees(key, part):
    key = jax.random.fold_in(key, 7)
    level_key, hot_key, spread_key = jax.random.split(key, 3)
    devices = BLOCKS // BLOCKS_DEV
    levels = jax.random.randint(level_key, (devices,), 0, SLOTS - 1)
    hottest = jax.random.randint(hot_key, (), 0, devices)
    levels = jnp.where(jnp.arange(devices) == hottest, SLOTS - 1, levels)
    rows = jnp.arange(BLOCKS)
    spread = jax.random.randint(spread_key, (BLOCKS,), 0, SLOTS)
    spread = jnp.where(rows == hottest * BLOCKS_DEV, SLOTS - 1, spread)
    return (1 + levels[rows // BLOCKS_DEV] * spread // (SLOTS - 1)).astype(jnp.int32)


def steps_of(stream_key, extent, cuts, smallest, largest):
    def one(axis_at, blocks):
        draws = jax.random.uniform(jax.random.fold_in(jax.random.fold_in(stream_key, 6), axis_at), (blocks,), jnp.float32, smallest / len(cuts), largest / len(cuts))
        return jnp.repeat(jnp.exp(draws), extent[axis_at] // blocks).reshape((-1,) + (1,) * (len(extent) - axis_at - 1))

    loudness = one(*cuts[0])
    for cut in cuts[1:]:
        loudness = loudness * one(*cut)
    return loudness


def scatter_about(key, dims, scale, most, shards=(), kind=jnp.bfloat16):
    result = scale * jax.random.normal(key, dims, jnp.float32)
    if shards:
        result = result * steps_of(key, dims, shards, -0.22, 0.18)
    return jnp.clip(result, -most, most).astype(kind)


def setup_inputs(seed: int = 0) -> dict:
    splits = jax.random.split(jax.random.key(seed), 9)
    node_features = scatter_about(splits[0], (WIDTH, NODES), 1.0, 6.0, ((0, 4), (1, 64)))
    weight_first = scatter_about(splits[1], (WIDTH, WIDTH), WIDTH ** -0.5, 0.25, ((0, 4),))
    weight_second = scatter_about(splits[2], (WIDTH, WIDTH), WIDTH ** -0.5, 0.25, ((0, 4),))
    tiles = scatter_about(splits[3], (BLOCKS, SLOTS, BLOCK, BLOCK), BLOCK ** -0.5, 0.375, ((0, 64),))
    slot_blocks = draw_slot_blocks(jax.random.fold_in(splits[8], 71), 0)
    degrees = draw_degrees(jax.random.fold_in(splits[8], 71), 0)
    block_position = draw_block_position(jax.random.fold_in(splits[8], 71), 0)
    cotangent = scatter_about(splits[7], (WIDTH, NODES), 1.0, 6.0, ((0, 4), (1, 64)))
    return {"node_features": node_features, "weight_first": weight_first, "weight_second": weight_second, "tiles": tiles, "slot_blocks": slot_blocks, "degrees": degrees, "block_position": block_position, "cotangent": cotangent}


def aggregate(values, tiles, position, degrees):
    width = values.shape[0]
    grouped = values.reshape(width, BLOCKS, BLOCK)
    slot_ids = jnp.arange(SLOTS)

    def one_row(args):
        row_tiles, row_positions, degree = args
        sources = grouped[:, row_positions, :].astype(jnp.float32)
        parts = jnp.einsum('fmk,mjk->mfj', sources, row_tiles.astype(jnp.float32), precision=lax.Precision.HIGHEST)
        weights = (slot_ids < degree).astype(jnp.float32)
        total = jnp.einsum('m,mfj->fj', weights, parts, precision=lax.Precision.HIGHEST)
        return total * lax.rsqrt(degree.astype(jnp.float32))
    rows = lax.map(one_row, (tiles, position, degrees))
    return jnp.transpose(rows, (1, 0, 2)).reshape(width, NODES)

def spread(gradient, tiles, position, degrees):
    width = gradient.shape[0]
    grouped = gradient.reshape(width, BLOCKS, BLOCK)
    slot_ids = jnp.arange(SLOTS)

    def one_row(row, total):
        row_grad = lax.dynamic_index_in_dim(grouped, row, 1, keepdims=False).astype(jnp.float32)
        row_tiles = lax.dynamic_index_in_dim(tiles, row, 0, keepdims=False).astype(jnp.float32)
        parts = jnp.einsum('fj,mjk->mfk', row_grad, row_tiles, precision=lax.Precision.HIGHEST)
        degree = degrees[row]
        weights = (slot_ids < degree).astype(jnp.float32) * lax.rsqrt(degree.astype(jnp.float32))
        parts = parts * weights[:, None, None]
        return total.at[:, position[row], :].add(jnp.transpose(parts, (1, 0, 2)))
    total = lax.fori_loop(0, BLOCKS, one_row, jnp.zeros((width, BLOCKS, BLOCK), jnp.float32))
    return total.reshape(width, NODES)

def mix(weights, features):
    quarter = WIDTH // N_REP
    total = jnp.zeros((WIDTH, NODES), jnp.float32)
    for group in range(N_REP):
        part = lax.dot_general(weights[group * quarter:(group + 1) * quarter], features[group * quarter:(group + 1) * quarter], (((0,), (0,)), ((), ())), preferred_element_type=jnp.float32)
        rounded = lax.optimization_barrier(part.astype(jnp.bfloat16))
        total = total + rounded.astype(jnp.float32)
    return total

def reference(node_features, weight_first, weight_second, tiles, slot_blocks, degrees, block_position, cotangent):
    position = block_position[slot_blocks]
    ax_rows = aggregate(node_features, tiles, position, degrees).astype(jnp.bfloat16)
    first = mix(weight_first, ax_rows)
    hidden = jax.nn.silu(first).astype(jnp.bfloat16)
    ah_rows = aggregate(hidden, tiles, position, degrees).astype(jnp.bfloat16)
    layer_output = mix(weight_second, ah_rows).astype(jnp.bfloat16)
    back = jnp.dot(weight_second, cotangent, preferred_element_type=jnp.float32).astype(jnp.bfloat16)
    factor = NODES ** (-0.5)
    grad_second = lax.dot_general(ah_rows, cotangent, (((1,), (1,)), ((), ())), preferred_element_type=jnp.float32) * factor
    spread_rows = spread(back, tiles, position, degrees)
    sigma = jax.nn.sigmoid(first)
    hidden_grad = (spread_rows * (sigma * (1.0 + first * (1.0 - sigma)))).astype(jnp.bfloat16)
    grad_first = lax.dot_general(ax_rows, hidden_grad, (((1,), (1,)), ((), ())), preferred_element_type=jnp.float32) * factor
    return (layer_output, grad_first, grad_second)
```

```python
import jax
import jax.numpy as jnp
from jax import lax
from jax.experimental import pallas as pl
from jax.experimental.pallas import tpu as pltpu
from jax.sharding import PartitionSpec as P

F32 = jnp.float32
BF16 = jnp.bfloat16
REACH = 2
SIDES = 2 * REACH + 1
HALO = (1, -1, 2, -2)


def behind(array, by):
    peers = lax.axis_size("blk")
    return lax.ppermute(array, "blk", [(i, (i + by) % peers) for i in range(peers)])


def across(array, flip):
    return lax.ppermute(array, "rep", [(i, i ^ flip) for i in range(lax.axis_size("rep"))])


def inverse_root(degree):
    value = jnp.float32(1.0)
    for count in range(2, 7):
        value = jnp.where(degree == count, jnp.float32(count**-0.5), value)
    return value


def place_of(slot_blocks, block_position, here, blocks, peers, row, slot):
    position = block_position[slot_blocks[row, slot]]
    side = lax.rem(position // blocks - here + REACH + peers, peers)
    return side * blocks + lax.rem(position, blocks)


def aggregate_kernel(
    peers,
    slot_blocks,
    degrees,
    block_position,
    *refs,
):
    held_refs, (tiles, weight, rows_out, keep_out, send_out, held, total) = refs[:SIDES], refs[SIDES:]
    blocks, slots, block, _ = tiles.shape
    here = lax.axis_index("blk")
    rank = lax.axis_index("rep")
    for side in range(SIDES):
        for inner in range(blocks):
            held[side * blocks + inner] = held_refs[side][:, inner * block : (inner + 1) * block]
    for row in range(blocks):
        degree = degrees[row]
        for slot in range(slots):

            def add(row=row, slot=slot):
                at = place_of(slot_blocks, block_position, here, blocks, peers, row, slot)
                part = lax.dot_general(
                    held[at],
                    tiles[row, slot],
                    (((1,), (1,)), ((), ())),
                    preferred_element_type=F32,
                )
                if slot == 0:
                    total[row] = part
                else:
                    total[row] += part

            if slot == 0:
                add()
            else:
                pl.when(slot < degree)(add)
        rows_out[:, row * block : (row + 1) * block] = (total[row] * inverse_root(degree)).astype(BF16)
    group = weight.shape[0] // 4
    rows = rows_out[...]
    for place, flip in enumerate((0, 2, 1, 3)):
        owner = rank ^ flip
        part = jnp.dot(
            weight[pl.ds(pl.multiple_of(owner * group, group), group), :],
            rows,
            preferred_element_type=F32,
        ).astype(BF16)
        out = keep_out if place < 2 else send_out
        out[(place % 2) * group : (place % 2 + 1) * group, :] = part


def spread_kernel(peers, slot_blocks, degrees, block_position, gradient, tiles, *refs):
    outs, total = refs[:SIDES], refs[SIDES]
    blocks, slots, block, _ = tiles.shape
    here = lax.axis_index("blk")
    total[...] = jnp.zeros_like(total)
    for row in range(blocks):
        degree = degrees[row]
        source = gradient[:, row * block : (row + 1) * block]
        for slot in range(slots):

            def add(row=row, slot=slot, degree=degree, source=source):
                at = place_of(slot_blocks, block_position, here, blocks, peers, row, slot)
                total[at] += jnp.dot(source, tiles[row, slot], preferred_element_type=F32) * inverse_root(degree)

            if slot == 0:
                add()
            else:
                pl.when(slot < degree)(add)
    for side in range(SIDES):
        for inner in range(blocks):
            outs[side][:, inner * block : (inner + 1) * block] = total[side * blocks + inner].astype(BF16)


SMEM = pl.BlockSpec(memory_space=pltpu.SMEM)
VMEM = pl.BlockSpec(memory_space=pltpu.VMEM)


def body(
    node_features,
    weight_first,
    weight_second,
    tiles,
    slot_blocks,
    degrees,
    block_position,
    cotangent,
):
    width, node_local = node_features.shape
    blocks, slots, block, _ = tiles.shape
    peers = lax.axis_size("blk")
    rank = lax.axis_index("rep")
    node_count = node_local * peers
    factor = node_count ** (-0.5)
    full = weight_first.shape[1]
    params = pltpu.CompilerParams(vmem_limit_bytes=40 * 1024 * 1024)
    cost = pl.CostEstimate(flops=2 * width * node_local * block * slots, bytes_accessed=8_000_000, transcendentals=0)

    def aggregate(held, weight_t):
        return pl.pallas_call(
            lambda *refs: aggregate_kernel(peers, *refs),
            out_shape=(
                jax.ShapeDtypeStruct((width, node_local), BF16),
                jax.ShapeDtypeStruct((full // 2, node_local), BF16),
                jax.ShapeDtypeStruct((full // 2, node_local), BF16),
            ),
            in_specs=[SMEM] * 3 + [VMEM] * (SIDES + 2),
            out_specs=(VMEM,) * 3,
            scratch_shapes=[
                pltpu.VMEM((SIDES * blocks, width, block), BF16),
                pltpu.VMEM((blocks, width, block), F32),
            ],
            compiler_params=params,
            cost_estimate=cost,
        )(slot_blocks, degrees, block_position, *held, tiles, weight_t)

    def halo(values):
        return [values if side == REACH else behind(values, REACH - side) for side in range(SIDES)]

    def scatter(keep, send):
        total = keep.astype(F32) + across(send, 1).astype(F32)
        other = across(total[width:].astype(BF16), 2)
        return total[:width] + other.astype(F32)

    def gather(own):
        pair = jnp.concatenate([own, across(own, 2)], axis=0)
        return jnp.concatenate([pair, across(pair, 1)], axis=0)

    def reduce_blk(term):
        parts = term.astype(BF16).reshape(width, 4, full // 4).transpose(1, 0, 2)
        parts = parts.reshape(peers, -1, full // 4)
        got = lax.all_to_all(parts, "blk", 0, 0, tiled=True)
        mine = jnp.sum(got.astype(F32), axis=0).astype(BF16)
        everyone = jnp.broadcast_to(mine[None], parts.shape)
        return lax.all_to_all(everyone, "blk", 0, 0, tiled=True).reshape(4, width, full // 4)

    def finish(groups):
        ordered = jnp.stack([lax.dynamic_index_in_dim(groups, relative_place(g), 0, keepdims=False) for g in range(4)], axis=1)
        return ordered.reshape(width, full).astype(F32) * factor

    def relative_place(group):
        flip = rank ^ group
        return (flip % 2) * 2 + flip // 2

    held_x = halo(node_features)
    parts = pl.pallas_call(
        lambda *refs: spread_kernel(peers, *refs),
        out_shape=(jax.ShapeDtypeStruct((width, node_local), BF16),) * SIDES,
        in_specs=[SMEM] * 3 + [VMEM] * 2,
        out_specs=(VMEM,) * SIDES,
        scratch_shapes=[pltpu.VMEM((SIDES * blocks, width, block), F32)],
        compiler_params=params,
        cost_estimate=cost,
    )(slot_blocks, degrees, block_position, cotangent, tiles)

    second_relative = jnp.concatenate(
        [lax.dynamic_slice_in_dim(weight_second, (rank ^ flip) * width, width, 1) for flip in (0, 2, 1, 3)], axis=1
    )
    ax_rows, keep, send = aggregate(held_x, weight_first.T)
    arrived = [parts[side] if side == REACH else behind(parts[side], side - REACH) for side in range(SIDES)]
    spread = sum(a.astype(F32) for a in arrived).astype(BF16)
    spread_all = gather(spread)
    spread_rows = jnp.dot(second_relative, spread_all, preferred_element_type=F32)

    first = scatter(keep, send)
    sigma = jax.nn.sigmoid(first)
    hidden = (first * sigma).astype(BF16)
    hidden_grad = (spread_rows * (sigma * (1.0 + first * (1.0 - sigma)))).astype(BF16)
    held_h = halo(hidden)
    _, keep_h, send_h = aggregate(held_h, weight_second.T)
    layer_output = scatter(keep_h, send_h).astype(BF16)

    term_second = lax.dot_general(hidden, spread_all, (((1,), (1,)), ((), ())), preferred_element_type=F32)
    term_first = lax.dot_general(ax_rows, gather(hidden_grad), (((1,), (1,)), ((), ())), preferred_element_type=F32)
    return layer_output, finish(reduce_blk(term_first)), finish(reduce_blk(term_second))


def solution(mesh):
    return jax.shard_map(
        body,
        mesh=mesh,
        in_specs=(
            P("rep", "blk"),
            P("rep", None),
            P("rep", None),
            P("blk", None, None, None),
            P("blk", None),
            P("blk"),
            P(),
            P("rep", "blk"),
        ),
        out_specs=(P("rep", "blk"), P("rep", None), P("rep", None)),
        check_vma=False,
    )
```

```python
import jax
import jax.numpy as jnp
from jax import lax
from jax.experimental import pallas as pl
from jax.experimental.pallas import tpu as pltpu
from jax.sharding import PartitionSpec as P

F32 = jnp.float32
BF16 = jnp.bfloat16
REACH = 2
SIDES = 2 * REACH + 1
FAR_FIRST = (0, 4, 1, 3)
FLIPS = (0, 2, 1, 3)


def behind(array, by):
    peers = lax.axis_size("blk")
    return lax.ppermute(array, "blk", [(i, (i + by) % peers) for i in range(peers)])


def across(array, flip):
    return lax.ppermute(array, "rep", [(i, i ^ flip) for i in range(lax.axis_size("rep"))])


def inverse_root(degree):
    value = jnp.float32(1.0)
    for count in range(2, 7):
        value = jnp.where(degree == count, jnp.float32(count**-0.5), value)
    return value


def place_of(slot_blocks, block_position, here, blocks, peers, row, slot):
    position = block_position[slot_blocks[row, slot]]
    side = lax.rem(position // blocks - here + REACH + peers, peers)
    return side * blocks + lax.rem(position, blocks)


def mix_rows(rank, weight, rows, keep_out, send_out):
    group = weight.shape[1] // 4
    for place, flip in enumerate(FLIPS):
        owner = rank ^ flip
        part = lax.dot_general(
            weight[:, pl.ds(pl.multiple_of(owner * group, group), group)],
            rows,
            (((0,), (0,)), ((), ())),
            preferred_element_type=F32,
        ).astype(BF16)
        out = keep_out if place < 2 else send_out
        out[(place % 2) * group : (place % 2 + 1) * group, :] = part


def gather_rows(peers, slot_blocks, degrees, block_position, tiles, held, total, rows_out):
    blocks, slots, block, _ = tiles.shape
    here = lax.axis_index("blk")
    for row in range(blocks):
        degree = degrees[row]
        for slot in range(slots):

            def add(row=row, slot=slot):
                at = place_of(slot_blocks, block_position, here, blocks, peers, row, slot)
                part = lax.dot_general(
                    held[at],
                    tiles[row, slot],
                    (((1,), (1,)), ((), ())),
                    preferred_element_type=F32,
                )
                if slot == 0:
                    total[row] = part
                else:
                    total[row] += part

            if slot == 0:
                add()
            else:
                pl.when(slot < degree)(add)
        rows_out[:, row * block : (row + 1) * block] = (total[row] * inverse_root(degree)).astype(BF16)


def join_kernel(ahead, back, part_ahead, part_back, join_ahead, join_back):
    width = ahead.shape[0]
    join_ahead[:width] = ahead[...]
    join_ahead[width:] = part_ahead[...]
    join_back[:width] = back[...]
    join_back[width:] = part_back[...]


def relay_kernel(part_ahead, part_back, far_ahead, far_back, sum_ahead, sum_back):
    width = sum_ahead.shape[0]
    sum_ahead[...] = (part_ahead[...].astype(F32) + far_ahead[width:].astype(F32)).astype(BF16)
    sum_back[...] = (part_back[...].astype(F32) + far_back[width:].astype(F32)).astype(BF16)


def add_kernel(part, came_ahead, came_back, spread):
    total = part[...].astype(F32) + came_ahead[...].astype(F32) + came_back[...].astype(F32)
    spread[...] = total.astype(BF16)


def first_kernel(peers, slot_blocks, degrees, block_position, *refs):
    far_ahead, near_ahead, own, near_back, far_back = refs[:5]
    tiles, weight, rows_out, keep_out, send_out, held, total = refs[5:]
    blocks, _, block, _ = tiles.shape
    width = own.shape[0]
    for side, ref in enumerate((far_ahead, near_ahead, own, near_back, far_back)):
        for inner in range(blocks):
            held[side * blocks + inner] = ref[:width, inner * block : (inner + 1) * block]
    gather_rows(peers, slot_blocks, degrees, block_position, tiles, held, total, rows_out)
    mix_rows(lax.axis_index("rep"), weight, rows_out[...], keep_out, send_out)


def second_kernel(peers, slot_blocks, degrees, block_position, *refs):
    held_refs, (tiles, weight, keep_out, send_out, held, total, rows) = refs[:SIDES], refs[SIDES:]
    blocks, _, block, _ = tiles.shape
    for side in range(SIDES):
        for inner in range(blocks):
            held[side * blocks + inner] = held_refs[side][:, inner * block : (inner + 1) * block]
    gather_rows(peers, slot_blocks, degrees, block_position, tiles, held, total, rows)
    mix_rows(lax.axis_index("rep"), weight, rows[...], keep_out, send_out)


def spread_kernel(peers, slot_blocks, degrees, block_position, gradient, tiles, *refs):
    outs, (gradient_in, tiles_in, total, sem, row_sems) = refs[:SIDES], refs[SIDES:]
    blocks, slots, block, _ = tiles.shape
    here = lax.axis_index("blk")
    copy = pltpu.make_async_copy(gradient, gradient_in, sem)
    rows = [pltpu.make_async_copy(tiles.at[row], tiles_in.at[row], row_sems.at[row]) for row in range(blocks)]
    for started in (copy, *rows):
        started.start()
    total[...] = jnp.zeros_like(total)
    copy.wait()
    for row in range(blocks):
        degree = degrees[row]
        source = gradient_in[:, row * block : (row + 1) * block]
        rows[row].wait()
        for slot in range(slots):

            def add(row=row, slot=slot, degree=degree, source=source):
                at = place_of(slot_blocks, block_position, here, blocks, peers, row, slot)
                total[at] += jnp.dot(source, tiles_in[row, slot], preferred_element_type=F32) * inverse_root(degree)

            if slot == 0:
                add()
            else:
                pl.when(slot < degree)(add)
    for side in range(SIDES):
        for inner in range(blocks):
            outs[side][:, inner * block : (inner + 1) * block] = total[side * blocks + inner].astype(BF16)


def settle_kernel(keep, came, mine, other):
    width = mine.shape[0]
    mine[...] = keep[:width].astype(F32) + came[:width].astype(F32)
    other[...] = (keep[width:].astype(F32) + came[width:].astype(F32)).astype(BF16)


def activate_kernel(mine, came, hidden, slope):
    first = mine[...] + came[: mine.shape[0]].astype(F32)
    sigma = 1.0 / (1.0 + jnp.exp(-first))
    hidden[...] = (first * sigma).astype(BF16)
    slope[...] = sigma * (1.0 + first * (1.0 - sigma))


def back_kernel(weight, slope, hidden, *refs):
    spread, (grad, term) = refs[:4], refs[4:]
    rank = lax.axis_index("rep")
    width = hidden.shape[0]
    total = None
    for place, flip in enumerate(FLIPS):
        owner = rank ^ flip
        part = jnp.dot(
            weight[:, pl.ds(pl.multiple_of(owner * width, width), width)],
            spread[place][...],
            preferred_element_type=F32,
        )
        total = part if place == 0 else total + part
    grad[...] = (total * slope[...]).astype(BF16)
    for place in range(4):
        term[place * width : (place + 1) * width] = lax.dot_general(
            hidden[...], spread[place][...], (((1,), (1,)), ((), ())), preferred_element_type=F32
        ).astype(BF16)


def outer_kernel(rows, term_second, *refs):
    grads, out = refs[:4], refs[4]
    width = rows.shape[0]
    for place in range(4):
        out[place * width : (place + 1) * width] = lax.dot_general(
            rows[...], grads[place][...], (((1,), (1,)), ((), ())), preferred_element_type=F32
        ).astype(BF16)
    out[4 * width :] = term_second[...]


def chunk_kernel(got, out):
    rows = 16
    total = got[:rows].astype(F32)
    for peer in range(1, got.shape[0] // rows):
        total += got[peer * rows : (peer + 1) * rows].astype(F32)
    block = total.astype(BF16)
    for peer in range(out.shape[0] // rows):
        out[peer * rows : (peer + 1) * rows] = block


def finish_kernel(factor, chunks, first, second):
    rank = lax.axis_index("rep")
    width = first.shape[0]
    for index, out in enumerate((first, second)):
        for place, flip in enumerate(FLIPS):
            at = index * 4 + place
            columns = pl.ds(pl.multiple_of((rank ^ flip) * width, width), width)
            out[:, columns] = chunks[at * width : (at + 1) * width].astype(F32) * factor


SMEM = pl.BlockSpec(memory_space=pltpu.SMEM)
VMEM = pl.BlockSpec(memory_space=pltpu.VMEM)
ANY = pl.BlockSpec(memory_space=pl.ANY)
MIB = 1024 * 1024


def body(
    node_features,
    weight_first,
    weight_second,
    tiles,
    slot_blocks,
    degrees,
    block_position,
    cotangent,
):
    width, node_local = node_features.shape
    blocks, slots, block, _ = tiles.shape
    peers = lax.axis_size("blk")
    factor = (node_local * peers) ** (-0.5)
    full = weight_first.shape[1]
    lists = (slot_blocks, degrees, block_position)
    node = jax.ShapeDtypeStruct((width, node_local), BF16)
    node_wide = jax.ShapeDtypeStruct((width, node_local), F32)
    half = jax.ShapeDtypeStruct((full // 2, node_local), BF16)

    def call(kernel, outs, in_specs, *args, scratch=(), out_specs=None, aliases={}, limit=12):
        return pl.pallas_call(
            kernel,
            out_shape=outs,
            in_specs=in_specs,
            out_specs=out_specs or jax.tree.map(lambda _: VMEM, outs),
            input_output_aliases=aliases,
            scratch_shapes=list(scratch),
            compiler_params=pltpu.CompilerParams(vmem_limit_bytes=limit * MIB),
            cost_estimate=pl.CostEstimate(flops=0, bytes_accessed=0, transcendentals=0),
        )(*args)

    def halo(values):
        held = {side: behind(values, REACH - side) for side in FAR_FIRST}
        held[REACH] = values
        return [held[side] for side in range(SIDES)]

    def gather(own, far):
        return own, far, across(own, 1), across(far, 1)

    pair = jax.ShapeDtypeStruct((2 * width, node_local), BF16)
    near_ahead = behind(node_features, 1)
    near_back = behind(node_features, -1)
    parts = call(
        lambda *refs: spread_kernel(peers, *refs),
        (node,) * SIDES,
        [SMEM] * 3 + [ANY] * 2,
        *lists,
        cotangent,
        tiles,
        scratch=[
            pltpu.VMEM((width, node_local), BF16),
            pltpu.VMEM(tiles.shape, BF16),
            pltpu.VMEM((SIDES * blocks, width, block), F32),
            pltpu.SemaphoreType.DMA,
            pltpu.SemaphoreType.DMA((blocks,)),
        ],
    )
    joined = call(join_kernel, (pair, pair), [VMEM] * 4, near_ahead, near_back, parts[4], parts[0])
    far_ahead, far_back = behind(joined[0], 1), behind(joined[1], -1)
    sums = call(relay_kernel, (node, node), [VMEM] * 4, parts[3], parts[1], far_ahead, far_back)
    came_ahead, came_back = behind(sums[0], 1), behind(sums[1], -1)
    held_scratch = [
        pltpu.VMEM((SIDES * blocks, width, block), BF16),
        pltpu.VMEM((blocks, width, block), F32),
    ]
    spread = call(add_kernel, node, [VMEM] * 3, parts[REACH], came_ahead, came_back)
    ax_rows, keep, send = call(
        lambda _, *refs: first_kernel(peers, *refs),
        (node, half, half),
        [ANY] + [SMEM] * 3 + [VMEM] * 7,
        spread,
        *lists,
        far_ahead,
        near_ahead,
        node_features,
        near_back,
        far_back,
        tiles,
        weight_first,
        scratch=held_scratch,
        limit=16,
    )
    mine, other = call(settle_kernel, (node_wide, node), [VMEM] * 2, keep, across(send, 1))
    came = across(other, 2)
    spread_all = gather(spread, across(spread, 2))
    hidden, slope = call(activate_kernel, (node, node_wide), [VMEM] * 2, mine, came)
    held_h = halo(hidden)
    hidden_grad, term_second = call(
        back_kernel,
        (node, jax.ShapeDtypeStruct((full, full // 4), BF16)),
        [VMEM] * 7,
        weight_second,
        slope,
        hidden,
        *spread_all,
    )
    stacked = jax.ShapeDtypeStruct((2 * full, full // 4), BF16)
    grad_all = gather(hidden_grad, across(hidden_grad, 2))
    terms = call(outer_kernel, stacked, [VMEM] * 6, ax_rows, term_second, *grad_all)
    got = lax.all_to_all(terms, "blk", 0, 0, tiled=True)
    chunks = call(chunk_kernel, stacked, [VMEM], got)
    everyone = lax.all_to_all(chunks, "blk", 0, 0, tiled=True)
    keep_h, send_h = call(
        lambda *refs: second_kernel(peers, *refs),
        (half, half),
        [SMEM] * 3 + [VMEM] * (SIDES + 2),
        *lists,
        *held_h,
        tiles,
        weight_second,
        scratch=[*held_scratch, pltpu.VMEM((width, node_local), BF16)],
    )
    mine_h, other_h = call(
        settle_kernel, (node_wide, node), [VMEM] * 2, keep_h, across(send_h, 1)
    )
    came_h = across(other_h, 2)
    layer_output = (mine_h + came_h.astype(F32)).astype(BF16)

    grad = jax.ShapeDtypeStruct((width, full), F32)
    first_out, second_out = call(lambda *refs: finish_kernel(factor, *refs), (grad, grad), [VMEM], everyone)
    return layer_output, first_out, second_out


def solution(mesh):
    return jax.shard_map(
        body,
        mesh=mesh,
        in_specs=(
            P("rep", "blk"),
            P("rep", None),
            P("rep", None),
            P("blk", None, None, None),
            P("blk", None),
            P("blk"),
            P(),
            P("rep", "blk"),
        ),
        out_specs=(P("rep", "blk"), P("rep", None), P("rep", None)),
        check_vma=False,
    )
```

```python
import jax
import jax.numpy as jnp
from jax import lax
from jax.experimental import pallas as pl
from jax.experimental.pallas import tpu as pltpu
from jax.sharding import PartitionSpec as P

F32 = jnp.float32
BF16 = jnp.bfloat16
REACH = 2
SIDES = 2 * REACH + 1
FLIPS = (0, 2, 1, 3)


def swap(array, step, turn):
    peers = lax.axis_size("blk")
    shift = step * turn
    return lax.ppermute(array, "blk", [(i, (((i + shift) ^ step) - shift) % peers) for i in range(peers)])


def sides_of(here, step):
    upward = lax.rem(here // step, 2) == 0
    first = jnp.where(upward, REACH + step, REACH - step)
    return first, 2 * REACH - first


def across(array, flip):
    return lax.ppermute(array, "rep", [(i, i ^ flip) for i in range(lax.axis_size("rep"))])


def inverse_root(degree):
    value = jnp.float32(1.0)
    for count in range(2, 7):
        value = jnp.where(degree == count, jnp.float32(count**-0.5), value)
    return value


def place_of(slot_blocks, block_position, here, blocks, peers, row, slot):
    position = block_position[slot_blocks[row, slot]]
    side = lax.rem(position // blocks - here + REACH + peers, peers)
    return side * blocks + lax.rem(position, blocks)


def mix_rows(rank, weight, rows, keep_out, send_out):
    group = weight.shape[1] // 4
    for place, flip in enumerate(FLIPS):
        owner = rank ^ flip
        part = lax.dot_general(
            weight[:, pl.ds(pl.multiple_of(owner * group, group), group)],
            rows,
            (((0,), (0,)), ((), ())),
            preferred_element_type=F32,
        ).astype(BF16)
        out = keep_out if place < 2 else send_out
        out[(place % 2) * group : (place % 2 + 1) * group, :] = part


def gather_rows(peers, slot_blocks, degrees, block_position, tiles, held, total, rows_out):
    blocks, slots, block, _ = tiles.shape
    here = lax.axis_index("blk")
    for row in range(blocks):
        degree = degrees[row]
        for slot in range(slots):

            def add(row=row, slot=slot):
                at = place_of(slot_blocks, block_position, here, blocks, peers, row, slot)
                part = lax.dot_general(
                    held[at],
                    tiles[row, slot],
                    (((1,), (1,)), ((), ())),
                    preferred_element_type=F32,
                )
                if slot == 0:
                    total[row] = part
                else:
                    total[row] += part

            if slot == 0:
                add()
            else:
                pl.when(slot < degree)(add)
        rows_out[:, row * block : (row + 1) * block] = (total[row] * inverse_root(degree)).astype(BF16)


def join_kernel(*refs):
    arrived, parts, joined = refs[:2], refs[2:4], refs[4:]
    width = arrived[0].shape[0]
    for turn in range(2):
        joined[turn][:width] = arrived[1 - turn][...]
        joined[turn][width:] = parts[turn][...]


def relay_kernel(*refs):
    parts, arrived, sums = refs[:2], refs[2:4], refs[4:]
    width = sums[0].shape[0]
    for turn in range(2):
        sums[turn][...] = (parts[turn][...].astype(F32) + arrived[1 - turn][width:].astype(F32)).astype(BF16)


def add_kernel(part, came_ahead, came_back, spread):
    total = part[...].astype(F32) + came_ahead[...].astype(F32) + came_back[...].astype(F32)
    spread[...] = total.astype(BF16)


def hold(held, own, pieces, blocks, block, far):
    here = lax.axis_index("blk")
    width = own.shape[0]
    ups = sides_of(here, 1)
    twos = (2 * ups[0] - REACH, 2 * ups[1] - REACH) if far else sides_of(here, 2)
    for side, ref in zip((REACH, *ups, *twos), (own, *pieces)):
        for inner in range(blocks):
            held[side * blocks + inner] = ref[:width, inner * block : (inner + 1) * block]


def first_kernel(peers, slot_blocks, degrees, block_position, *refs):
    own, pieces = refs[0], refs[1:5]
    tiles, weight, rows_out, keep_out, send_out, held, total = refs[5:]
    blocks, _, block, _ = tiles.shape
    width = own.shape[0]
    hold(held, own, pieces, blocks, block, far=True)
    gather_rows(peers, slot_blocks, degrees, block_position, tiles, held, total, rows_out)
    mix_rows(lax.axis_index("rep"), weight, rows_out[...], keep_out, send_out)


def second_kernel(peers, slot_blocks, degrees, block_position, *refs):
    held_refs, (tiles, weight, keep_out, send_out, held, total, rows) = refs[:SIDES], refs[SIDES:]
    blocks, _, block, _ = tiles.shape
    hold(held, held_refs[0], held_refs[1:], blocks, block, far=False)
    gather_rows(peers, slot_blocks, degrees, block_position, tiles, held, total, rows)
    mix_rows(lax.axis_index("rep"), weight, rows[...], keep_out, send_out)


def spread_kernel(peers, slot_blocks, degrees, block_position, gradient, tiles, *refs):
    outs, (gradient_in, tiles_in, total, sem, row_sems) = refs[:SIDES], refs[SIDES:]
    blocks, slots, block, _ = tiles.shape
    here = lax.axis_index("blk")
    copy = pltpu.make_async_copy(gradient, gradient_in, sem)
    rows = [pltpu.make_async_copy(tiles.at[row], tiles_in.at[row], row_sems.at[row]) for row in range(blocks)]
    for started in (copy, *rows):
        started.start()
    total[...] = jnp.zeros_like(total)
    copy.wait()
    for row in range(blocks):
        degree = degrees[row]
        source = gradient_in[:, row * block : (row + 1) * block]
        rows[row].wait()
        for slot in range(slots):

            def add(row=row, slot=slot, degree=degree, source=source):
                at = place_of(slot_blocks, block_position, here, blocks, peers, row, slot)
                total[at] += jnp.dot(source, tiles_in[row, slot], preferred_element_type=F32) * inverse_root(degree)

            if slot == 0:
                add()
            else:
                pl.when(slot < degree)(add)
    ups = sides_of(here, 1)
    sides = (REACH, *ups, 2 * ups[0] - REACH, 2 * ups[1] - REACH)
    for side, out in zip(sides, outs):
        for inner in range(blocks):
            out[:, inner * block : (inner + 1) * block] = total[side * blocks + inner].astype(BF16)


def settle_kernel(keep, came, mine, other):
    width = mine.shape[0]
    mine[...] = keep[:width].astype(F32) + came[:width].astype(F32)
    other[...] = (keep[width:].astype(F32) + came[width:].astype(F32)).astype(BF16)


def activate_kernel(mine, came, hidden, slope):
    first = mine[...] + came[: mine.shape[0]].astype(F32)
    sigma = 1.0 / (1.0 + jnp.exp(-first))
    hidden[...] = (first * sigma).astype(BF16)
    slope[...] = sigma * (1.0 + first * (1.0 - sigma))


def back_kernel(weight, slope, hidden, *refs):
    spread, (grad, term) = refs[:4], refs[4:]
    rank = lax.axis_index("rep")
    width = hidden.shape[0]
    total = None
    for place, flip in enumerate(FLIPS):
        owner = rank ^ flip
        part = jnp.dot(
            weight[:, pl.ds(pl.multiple_of(owner * width, width), width)],
            spread[place][...],
            preferred_element_type=F32,
        )
        total = part if place == 0 else total + part
    grad[...] = (total * slope[...]).astype(BF16)
    for place in range(4):
        term[place * width : (place + 1) * width] = lax.dot_general(
            hidden[...], spread[place][...], (((1,), (1,)), ((), ())), preferred_element_type=F32
        ).astype(BF16)


def outer_kernel(rows, term_second, *refs):
    grads, out = refs[:4], refs[4]
    width = rows.shape[0]
    for place in range(4):
        out[place * width : (place + 1) * width] = lax.dot_general(
            rows[...], grads[place][...], (((1,), (1,)), ((), ())), preferred_element_type=F32
        ).astype(BF16)
    out[4 * width :] = term_second[...]


def chunk_kernel(got, out):
    rows = 16
    total = got[:rows].astype(F32)
    for peer in range(1, got.shape[0] // rows):
        total += got[peer * rows : (peer + 1) * rows].astype(F32)
    block = total.astype(BF16)
    for peer in range(out.shape[0] // rows):
        out[peer * rows : (peer + 1) * rows] = block


def finish_kernel(factor, chunks, first, second):
    rank = lax.axis_index("rep")
    width = first.shape[0]
    for index, out in enumerate((first, second)):
        for place, flip in enumerate(FLIPS):
            at = index * 4 + place
            columns = pl.ds(pl.multiple_of((rank ^ flip) * width, width), width)
            out[:, columns] = chunks[at * width : (at + 1) * width].astype(F32) * factor


SMEM = pl.BlockSpec(memory_space=pltpu.SMEM)
VMEM = pl.BlockSpec(memory_space=pltpu.VMEM)
ANY = pl.BlockSpec(memory_space=pl.ANY)
MIB = 1024 * 1024


def body(
    node_features,
    weight_first,
    weight_second,
    tiles,
    slot_blocks,
    degrees,
    block_position,
    cotangent,
):
    width, node_local = node_features.shape
    blocks, slots, block, _ = tiles.shape
    peers = lax.axis_size("blk")
    factor = (node_local * peers) ** (-0.5)
    full = weight_first.shape[1]
    lists = (slot_blocks, degrees, block_position)
    node = jax.ShapeDtypeStruct((width, node_local), BF16)
    node_wide = jax.ShapeDtypeStruct((width, node_local), F32)
    half = jax.ShapeDtypeStruct((full // 2, node_local), BF16)

    def call(kernel, outs, in_specs, *args, scratch=(), out_specs=None, aliases={}, limit=12):
        return pl.pallas_call(
            kernel,
            out_shape=outs,
            in_specs=in_specs,
            out_specs=out_specs or jax.tree.map(lambda _: VMEM, outs),
            input_output_aliases=aliases,
            scratch_shapes=list(scratch),
            compiler_params=pltpu.CompilerParams(vmem_limit_bytes=limit * MIB),
            cost_estimate=pl.CostEstimate(flops=0, bytes_accessed=0, transcendentals=0),
        )(*args)

    def gather(own, far):
        return own, far, across(own, 1), across(far, 1)

    pair = jax.ShapeDtypeStruct((2 * width, node_local), BF16)
    near = [swap(node_features, 1, turn) for turn in range(2)]
    parts = call(
        lambda *refs: spread_kernel(peers, *refs),
        (node,) * SIDES,
        [SMEM] * 3 + [ANY] * 2,
        *lists,
        cotangent,
        tiles,
        scratch=[
            pltpu.VMEM((width, node_local), BF16),
            pltpu.VMEM(tiles.shape, BF16),
            pltpu.VMEM((SIDES * blocks, width, block), F32),
            pltpu.SemaphoreType.DMA,
            pltpu.SemaphoreType.DMA((blocks,)),
        ],
    )
    joined = call(join_kernel, (pair, pair), [VMEM] * 4, *near, *parts[3:])
    far = [swap(joined[turn], 1, turn) for turn in range(2)]
    sums = call(relay_kernel, (node, node), [VMEM] * 4, *parts[1:3], *far)
    came_parts = [swap(sums[turn], 1, turn) for turn in range(2)]
    held_scratch = [
        pltpu.VMEM((SIDES * blocks, width, block), BF16),
        pltpu.VMEM((blocks, width, block), F32),
    ]
    spread = call(add_kernel, node, [VMEM] * 3, parts[0], *came_parts)
    ax_rows, keep, send = call(
        lambda _, *refs: first_kernel(peers, *refs),
        (node, half, half),
        [ANY] + [SMEM] * 3 + [VMEM] * 7,
        spread,
        *lists,
        node_features,
        *near,
        *far,
        tiles,
        weight_first,
        scratch=held_scratch,
        limit=16,
    )
    mine, other = call(settle_kernel, (node_wide, node), [VMEM] * 2, keep, across(send, 1))
    came = across(other, 2)
    spread_all = gather(spread, across(spread, 2))
    hidden, slope = call(activate_kernel, (node, node_wide), [VMEM] * 2, mine, came)
    held_h = (hidden, *(swap(hidden, step, turn) for step in (1, 2) for turn in range(2)))
    hidden_grad, term_second = call(
        back_kernel,
        (node, jax.ShapeDtypeStruct((full, full // 4), BF16)),
        [VMEM] * 7,
        weight_second,
        slope,
        hidden,
        *spread_all,
    )
    stacked = jax.ShapeDtypeStruct((2 * full, full // 4), BF16)
    grad_all = gather(hidden_grad, across(hidden_grad, 2))
    terms = call(outer_kernel, stacked, [VMEM] * 6, ax_rows, term_second, *grad_all)
    got = lax.all_to_all(terms, "blk", 0, 0, tiled=True)
    chunks = call(chunk_kernel, stacked, [VMEM], got)
    everyone = lax.all_to_all(chunks, "blk", 0, 0, tiled=True)
    keep_h, send_h = call(
        lambda *refs: second_kernel(peers, *refs),
        (half, half),
        [SMEM] * 3 + [VMEM] * (SIDES + 2),
        *lists,
        *held_h,
        tiles,
        weight_second,
        scratch=[*held_scratch, pltpu.VMEM((width, node_local), BF16)],
    )
    mine_h, other_h = call(
        settle_kernel, (node_wide, node), [VMEM] * 2, keep_h, across(send_h, 1)
    )
    came_h = across(other_h, 2)
    layer_output = (mine_h + came_h.astype(F32)).astype(BF16)

    grad = jax.ShapeDtypeStruct((width, full), F32)
    first_out, second_out = call(lambda *refs: finish_kernel(factor, *refs), (grad, grad), [VMEM], everyone)
    return layer_output, first_out, second_out


def solution(mesh):
    return jax.shard_map(
        body,
        mesh=mesh,
        in_specs=(
            P("rep", "blk"),
            P("rep", None),
            P("rep", None),
            P("blk", None, None, None),
            P("blk", None),
            P("blk"),
            P(),
            P("rep", "blk"),
        ),
        out_specs=(P("rep", "blk"), P("rep", None), P("rep", None)),
        check_vma=False,
    )
```

```python
import jax
import jax.numpy as jnp
from jax import lax
from jax.experimental import pallas as pl
from jax.experimental.pallas import tpu as pltpu
from jax.sharding import PartitionSpec as P

F32 = jnp.float32
BF16 = jnp.bfloat16
REACH = 2
SIDES = 2 * REACH + 1
FLIPS = (0, 2, 1, 3)


def swap(array, step, turn):
    peers = lax.axis_size("blk")
    shift = step * turn
    return lax.ppermute(array, "blk", [(i, (((i + shift) ^ step) - shift) % peers) for i in range(peers)])


def sides_of(here, step):
    upward = lax.rem(here // step, 2) == 0
    first = jnp.where(upward, REACH + step, REACH - step)
    return first, 2 * REACH - first


def across(array, flip):
    return lax.ppermute(array, "rep", [(i, i ^ flip) for i in range(lax.axis_size("rep"))])


def inverse_root(degree):
    value = jnp.float32(1.0)
    for count in range(2, 7):
        value = jnp.where(degree == count, jnp.float32(count**-0.5), value)
    return value


def place_of(slot_blocks, block_position, here, blocks, peers, row, slot):
    position = block_position[slot_blocks[row, slot]]
    side = lax.rem(position // blocks - here + REACH + peers, peers)
    return side * blocks + lax.rem(position, blocks)


def mix_rows(rank, weight, rows, keep_out, send_out):
    group = weight.shape[1] // 4
    for place, flip in enumerate(FLIPS):
        owner = rank ^ flip
        part = lax.dot_general(
            weight[:, pl.ds(pl.multiple_of(owner * group, group), group)],
            rows,
            (((0,), (0,)), ((), ())),
            preferred_element_type=F32,
        ).astype(BF16)
        out = keep_out if place < 2 else send_out
        out[(place % 2) * group : (place % 2 + 1) * group, :] = part


def gather_rows(peers, slot_blocks, degrees, block_position, tiles, held, total, rows_out):
    blocks, slots, block, _ = tiles.shape
    here = lax.axis_index("blk")
    for row in range(blocks):
        degree = degrees[row]
        for slot in range(slots):

            def add(row=row, slot=slot):
                at = place_of(slot_blocks, block_position, here, blocks, peers, row, slot)
                part = lax.dot_general(
                    held[at],
                    tiles[row, slot],
                    (((1,), (1,)), ((), ())),
                    preferred_element_type=F32,
                )
                if slot == 0:
                    total[row] = part
                else:
                    total[row] += part

            if slot == 0:
                add()
            else:
                pl.when(slot < degree)(add)
        rows_out[:, row * block : (row + 1) * block] = (total[row] * inverse_root(degree)).astype(BF16)


def join_kernel(*refs):
    arrived, parts, joined = refs[:2], refs[2:4], refs[4:]
    width = arrived[0].shape[0]
    for turn in range(2):
        joined[turn][:width] = arrived[1 - turn][...]
        joined[turn][width:] = parts[turn][...]


def relay_kernel(*refs):
    parts, arrived, sums = refs[:2], refs[2:4], refs[4:]
    width = sums[0].shape[0]
    for turn in range(2):
        sums[turn][...] = (parts[turn][...].astype(F32) + arrived[1 - turn][width:].astype(F32)).astype(BF16)


def add_kernel(part, came_ahead, came_back, spread):
    total = part[...].astype(F32) + came_ahead[...].astype(F32) + came_back[...].astype(F32)
    spread[...] = total.astype(BF16)


def hold(held, own, pieces, blocks, block, far):
    here = lax.axis_index("blk")
    width = own.shape[0]
    ups = sides_of(here, 1)
    twos = (2 * ups[0] - REACH, 2 * ups[1] - REACH) if far else sides_of(here, 2)
    for side, ref in zip((REACH, *ups, *twos), (own, *pieces)):
        for inner in range(blocks):
            held[side * blocks + inner] = ref[:width, inner * block : (inner + 1) * block]


def first_kernel(peers, slot_blocks, degrees, block_position, *refs):
    own, pieces = refs[0], refs[1:5]
    tiles, weight, rows_out, keep_out, send_out, held, total = refs[5:]
    blocks, _, block, _ = tiles.shape
    width = own.shape[0]
    hold(held, own, pieces, blocks, block, far=True)
    gather_rows(peers, slot_blocks, degrees, block_position, tiles, held, total, rows_out)
    mix_rows(lax.axis_index("rep"), weight, rows_out[...], keep_out, send_out)


def second_kernel(peers, slot_blocks, degrees, block_position, *refs):
    held_refs, (tiles, weight, keep_out, send_out, held, total, rows) = refs[:SIDES], refs[SIDES:]
    blocks, _, block, _ = tiles.shape
    hold(held, held_refs[0], held_refs[1:], blocks, block, far=False)
    gather_rows(peers, slot_blocks, degrees, block_position, tiles, held, total, rows)
    mix_rows(lax.axis_index("rep"), weight, rows[...], keep_out, send_out)


def spread_kernel(peers, slot_blocks, degrees, block_position, gradient, tiles, *refs):
    outs, (gradient_in, tiles_in, total, sem, row_sems) = refs[:SIDES], refs[SIDES:]
    blocks, slots, block, _ = tiles.shape
    here = lax.axis_index("blk")
    copy = pltpu.make_async_copy(gradient, gradient_in, sem)
    rows = [pltpu.make_async_copy(tiles.at[row], tiles_in.at[row], row_sems.at[row]) for row in range(blocks)]
    for started in (copy, *rows):
        started.start()
    total[...] = jnp.zeros_like(total)
    copy.wait()
    for row in range(blocks):
        degree = degrees[row]
        source = gradient_in[:, row * block : (row + 1) * block]
        rows[row].wait()
        for slot in range(slots):

            def add(row=row, slot=slot, degree=degree, source=source):
                at = place_of(slot_blocks, block_position, here, blocks, peers, row, slot)
                total[at] += jnp.dot(source, tiles_in[row, slot], preferred_element_type=F32) * inverse_root(degree)

            if slot == 0:
                add()
            else:
                pl.when(slot < degree)(add)
    ups = sides_of(here, 1)
    sides = (REACH, *ups, 2 * ups[0] - REACH, 2 * ups[1] - REACH)
    for side, out in zip(sides, outs):
        for inner in range(blocks):
            out[:, inner * block : (inner + 1) * block] = total[side * blocks + inner].astype(BF16)


def settle_kernel(keep, came, mine, other):
    width = mine.shape[0]
    mine[...] = keep[:width].astype(F32) + came[:width].astype(F32)
    other[...] = (keep[width:].astype(F32) + came[width:].astype(F32)).astype(BF16)


def activate_kernel(mine, came, hidden, slope):
    first = mine[...] + came[: mine.shape[0]].astype(F32)
    sigma = 1.0 / (1.0 + jnp.exp(-first))
    hidden[...] = (first * sigma).astype(BF16)
    slope[...] = sigma * (1.0 + first * (1.0 - sigma))


def back_kernel(weight, slope, hidden, *refs):
    spread, (grad, term) = refs[:4], refs[4:]
    rank = lax.axis_index("rep")
    width = hidden.shape[0]
    total = None
    for place, flip in enumerate(FLIPS):
        owner = rank ^ flip
        part = jnp.dot(
            weight[:, pl.ds(pl.multiple_of(owner * width, width), width)],
            spread[place][...],
            preferred_element_type=F32,
        )
        total = part if place == 0 else total + part
    grad[...] = (total * slope[...]).astype(BF16)
    for place in range(4):
        term[place * width : (place + 1) * width] = lax.dot_general(
            hidden[...], spread[place][...], (((1,), (1,)), ((), ())), preferred_element_type=F32
        ).astype(BF16)


def outer_kernel(rows, term_second, *refs):
    grads, out = refs[:4], refs[4]
    width = rows.shape[0]
    for place in range(4):
        out[place * width : (place + 1) * width] = lax.dot_general(
            rows[...], grads[place][...], (((1,), (1,)), ((), ())), preferred_element_type=F32
        ).astype(BF16)
    out[4 * width :] = term_second[...]


def chunk_kernel(got, out):
    rows = 16
    total = got[:rows].astype(F32)
    for peer in range(1, got.shape[0] // rows):
        total += got[peer * rows : (peer + 1) * rows].astype(F32)
    block = total.astype(BF16)
    for peer in range(out.shape[0] // rows):
        out[peer * rows : (peer + 1) * rows] = block


def finish_kernel(factor, chunks, first, second):
    rank = lax.axis_index("rep")
    width = first.shape[0]
    for index, out in enumerate((first, second)):
        for place, flip in enumerate(FLIPS):
            at = index * 4 + place
            columns = pl.ds(pl.multiple_of((rank ^ flip) * width, width), width)
            out[:, columns] = chunks[at * width : (at + 1) * width].astype(F32) * factor


SMEM = pl.BlockSpec(memory_space=pltpu.SMEM)
VMEM = pl.BlockSpec(memory_space=pltpu.VMEM)
ANY = pl.BlockSpec(memory_space=pl.ANY)
MIB = 1024 * 1024


def body(
    node_features,
    weight_first,
    weight_second,
    tiles,
    slot_blocks,
    degrees,
    block_position,
    cotangent,
):
    width, node_local = node_features.shape
    blocks, slots, block, _ = tiles.shape
    peers = lax.axis_size("blk")
    factor = (node_local * peers) ** (-0.5)
    full = weight_first.shape[1]
    lists = (slot_blocks, degrees, block_position)
    node = jax.ShapeDtypeStruct((width, node_local), BF16)
    node_wide = jax.ShapeDtypeStruct((width, node_local), F32)
    half = jax.ShapeDtypeStruct((full // 2, node_local), BF16)

    def call(kernel, outs, in_specs, *args, scratch=(), out_specs=None, aliases={}, limit=12):
        return pl.pallas_call(
            kernel,
            out_shape=outs,
            in_specs=in_specs,
            out_specs=out_specs or jax.tree.map(lambda _: VMEM, outs),
            input_output_aliases=aliases,
            scratch_shapes=list(scratch),
            compiler_params=pltpu.CompilerParams(vmem_limit_bytes=limit * MIB),
            cost_estimate=pl.CostEstimate(flops=0, bytes_accessed=0, transcendentals=0),
        )(*args)

    def gather(own, far):
        return own, far, across(own, 1), across(far, 1)

    pair = jax.ShapeDtypeStruct((2 * width, node_local), BF16)
    near = [swap(node_features, 1, turn) for turn in range(2)]
    parts = call(
        lambda *refs: spread_kernel(peers, *refs),
        (node,) * SIDES,
        [SMEM] * 3 + [ANY] * 2,
        *lists,
        cotangent,
        tiles,
        scratch=[
            pltpu.VMEM((width, node_local), BF16),
            pltpu.VMEM(tiles.shape, BF16),
            pltpu.VMEM((SIDES * blocks, width, block), F32),
            pltpu.SemaphoreType.DMA,
            pltpu.SemaphoreType.DMA((blocks,)),
        ],
    )
    joined = call(join_kernel, (pair, pair), [VMEM] * 4, *near, *parts[3:])
    far = [swap(joined[turn], 1, turn) for turn in range(2)]
    sums = call(relay_kernel, (node, node), [VMEM] * 4, *parts[1:3], *far)
    came_parts = [swap(sums[turn], 1, turn) for turn in range(2)]
    held_scratch = [
        pltpu.VMEM((SIDES * blocks, width, block), BF16),
        pltpu.VMEM((blocks, width, block), F32),
    ]
    spread = call(add_kernel, node, [VMEM] * 3, parts[0], *came_parts)
    ax_rows, keep, send = call(
        lambda *refs: first_kernel(peers, *refs),
        (node, half, half),
        [SMEM] * 3 + [VMEM] * 7,
        *lists,
        node_features,
        *near,
        *far,
        tiles,
        weight_first,
        scratch=held_scratch,
        limit=16,
    )
    mine, other = call(settle_kernel, (node_wide, node), [VMEM] * 2, keep, across(send, 1))
    came = across(other, 2)
    spread_all = gather(spread, across(spread, 2))
    hidden, slope = call(activate_kernel, (node, node_wide), [VMEM] * 2, mine, came)
    held_h = (hidden, *(swap(hidden, step, turn) for step in (1, 2) for turn in range(2)))
    hidden_grad, term_second = call(
        back_kernel,
        (node, jax.ShapeDtypeStruct((full, full // 4), BF16)),
        [VMEM] * 7,
        weight_second,
        slope,
        hidden,
        *spread_all,
    )
    stacked = jax.ShapeDtypeStruct((2 * full, full // 4), BF16)
    grad_all = gather(hidden_grad, across(hidden_grad, 2))
    terms = call(outer_kernel, stacked, [VMEM] * 6, ax_rows, term_second, *grad_all)
    got = lax.all_to_all(terms, "blk", 0, 0, tiled=True)
    chunks = call(chunk_kernel, stacked, [VMEM], got)
    everyone = lax.all_to_all(chunks, "blk", 0, 0, tiled=True)
    keep_h, send_h = call(
        lambda *refs: second_kernel(peers, *refs),
        (half, half),
        [SMEM] * 3 + [VMEM] * (SIDES + 2),
        *lists,
        *held_h,
        tiles,
        weight_second,
        scratch=[*held_scratch, pltpu.VMEM((width, node_local), BF16)],
    )
    mine_h, other_h = call(
        settle_kernel, (node_wide, node), [VMEM] * 2, keep_h, across(send_h, 1)
    )
    came_h = across(other_h, 2)
    layer_output = (mine_h + came_h.astype(F32)).astype(BF16)

    grad = jax.ShapeDtypeStruct((width, full), F32)
    first_out, second_out = call(lambda *refs: finish_kernel(factor, *refs), (grad, grad), [VMEM], everyone)
    return layer_output, first_out, second_out


def solution(mesh):
    return jax.shard_map(
        body,
        mesh=mesh,
        in_specs=(
            P("rep", "blk"),
            P("rep", None),
            P("rep", None),
            P("blk", None, None, None),
            P("blk", None),
            P("blk"),
            P(),
            P("rep", "blk"),
        ),
        out_specs=(P("rep", "blk"), P("rep", None), P("rep", None)),
        check_vma=False,
    )
```
